32 devices in a mesh: grp: 4 (over y, x), blk: 8 (over z, core).
Axes of the slice: x: 2, y: 2, z: 4, core: 2. Of those that a mesh axis runs over, the one named last changes fastest.
Arguments:
- inv_factor: bfloat16 [192, 384, 384], P(('grp', 'blk')), may hold values from -0.3125 to 0.3125
- coupling: bfloat16 [192, 384, 768], P(('grp', 'blk')), may hold values from -0.75 to 0.75
- boundary: bfloat16 [192, 768, 768], P(('grp', 'blk')), may hold values from -6 to 6
- load_int: bfloat16 [192, 384], P(('grp', 'blk')), may hold values from -6 to 6
- load_bnd: bfloat16 [192, 768], P(('grp', 'blk')), may hold values from -6 to 6
- counts: int32 [32], P(('grp', 'blk')), may hold values from 1 to 6, 128 in all
- tile_owner: int32 [192, 36, 1], P(('grp', 'blk')), may hold values from 0 to 31; in each aligned block of 216 rows (0 to 215, 216 to 431, ..., all dimensions but the last counted through in order) at most 10 rows name the same one
- tile_slot: int32 [192, 36], P(('grp', 'blk')), may hold values from 0 to 63
- vec_owner: int32 [192, 6, 1], P(('grp', 'blk')), may hold values from 0 to 31; in each aligned block of 36 rows (0 to 35, 36 to 71, ..., all dimensions but the last counted through in order) at most 2 rows name the same one
- vec_slot: int32 [192, 6], P(('grp', 'blk')), may hold values from 0 to 15
Outputs:
- assembled: float32 [2048, 128, 128], P(('grp', 'blk'))
- loads: float32 [512, 128], P(('grp', 'blk'))
The draws below stay inside these ranges and needn't reach their ends.
Inputs may be any that keep to these rules, and one draw needn't show every extreme that they name: `tile_owner`: among the 216 rows of one device, no owner is named by more than 10 tiles. `vec_owner`: among the 36 rows of one device, no owner is named by more than 2 load blocks.
All inputs are finite; a program needn't handle non-finite values. No bound on the sum of `counts` on one device may be relied on, other than what follows from the above.
Results may differ from the reference program's by a relative error of at most 0.004.
Values may be sent and summed in bfloat16 or wider, within the bound.
A program may use at most 128 MiB of HBM per device.

```python
import math
import jax
import jax.numpy as jnp
import numpy as np
from jax import lax

NI = 384
BLOCK_UNKNOWNS = 128
TILES = 6
EMAX = 6
SLOT_DEV = 64
NB = 768
ETILES = 216
LIVE = 4
CAP = 10
VCAP = 2
VSLOT_DEV = 16
ELEMS = 192
INTERFACE_TILES = 2048
LOAD_BLOCK_COUNT = 512
DEVICES = 32


def with_ends(result, rng, least, top_value):
    dims = result.shape
    spot = [jax.random.randint(jax.random.fold_in(rng, axis), (), 0, dims[axis]) for axis in range(len(dims))]
    result = result.at[tuple(spot)].set(least)
    longest = dims.index(max(dims))
    spot[longest] = (spot[longest] + 1) % dims[longest]
    return result.at[tuple(spot)].set(top_value)


def block_scale(key, dims, split, least, top_value):
    loudness = 1.0
    for axis_at, shards_of in split:
        draws = jax.random.uniform(jax.random.fold_in(jax.random.fold_in(key, 6), axis_at), (shards_of,), jnp.float32, least / len(split), top_value / len(split))
        loudness = loudness * jnp.repeat(jnp.exp(draws), dims[axis_at] // shards_of).reshape((-1,) + (1,) * (len(dims) - 1 - axis_at))
    return loudness


def profile(number_of, total, most, lean):
    loads = [(1 << 20) // math.isqrt(grade ** lean) + 1 for grade in range(2, number_of + 1)]
    spare, given = total - most - (number_of - 1), [1] * (number_of - 1)
    while spare > 0:
        free = [i for i in range(number_of - 1) if given[i] < most]
        pool, remaining = sum([loads[i] for i in free]), spare
        for i in free:
            more = min(most - given[i], max(1, remaining * loads[i] // pool), spare)
            given[i] = given[i] + more
            spare = spare - more
    return np.array([most] + given)


def ragged_sizes(rng, count, total, most, skew):
    if count == 2:
        one = jax.random.randint(rng, (), max(1, total - most), min(most, total - 1) + 1)
        return jnp.stack([one, total - one])
    lengths = jnp.asarray(profile(count, total, most, skew), jnp.int32)
    twos = (count - 1) // 2
    donor, taker = lengths[1:1 + 2 * twos:2], lengths[2:2 + 2 * twos:2]
    margin = jnp.minimum(donor - 1, most - taker)
    passed = jax.random.randint(jax.random.fold_in(rng, 1), (twos,), 0, 1 << 20) % (margin + 1)
    lengths = lengths.at[1:1 + 2 * twos:2].set(donor - passed).at[2:2 + 2 * twos:2].set(taker + passed)
    return lengths[jax.random.permutation(jax.random.fold_in(rng, 2), count)]


def deal_out(stream_key, own, number, rows, amount, top, reach, lean):
    order = jax.random.permutation(stream_key, amount)
    packed, usual = portions_of(amount, rows * top, reach, lean, True), portions_of(amount, rows * top, reach, lean, False)
    places = jnp.arange(amount)

    def named(lengths, rotation):
        used = int((lengths > 0).sum())
        fixed = max(1, used // 4)
        shifted = fixed + (places - fixed + rotation * (used - fixed)) % max(1, amount - fixed)
        return jnp.zeros((amount,), jnp.int32).at[order[jnp.where(places < fixed, places, shifted)]].set(jnp.asarray(lengths, jnp.int32))

    lengths = jnp.where(number % 4 == 0, named(packed, number // 4), named(usual, number - number // 4 - 1))
    mixed = jax.random.permutation(jax.random.fold_in(own, 3), amount)
    donor, taker = mixed[0:amount // 2 * 2:2], mixed[1:amount // 2 * 2:2]
    margin = jnp.minimum(lengths[donor] - 1, reach - lengths[taker]) // 2
    margin = jnp.where((donor == order[0]) | (taker == order[0]) | (lengths[taker] == 0), 0, jnp.maximum(margin, 0))
    shifted = jax.random.randint(jax.random.fold_in(own, 4), (amount // 2,), 0, 1 << 20) % (margin + 1)
    lengths = lengths.at[donor].add(-shifted).at[taker].add(shifted)
    labels = jnp.searchsorted(jnp.cumsum(lengths), jnp.arange(rows * top), side="right").astype(jnp.int32)
    listing = labels.reshape(top, rows).T
    listing = listing[jax.random.permutation(jax.random.fold_in(own, 1), rows)]
    rotation = jax.random.randint(jax.random.fold_in(own, 2), (rows, 1), 0, top)
    return jnp.take_along_axis(listing, (jnp.arange(top)[None, :] + rotation) % top, axis=1)


def portions_of(number_of, total, most, slope, full):
    loads = [(1 << 20) // math.isqrt(standing ** slope) + 1 for standing in range(1, number_of + 1)]
    largest = most if full else min(most, max(-(-total // number_of), total * loads[0] // sum(loads)))
    least = 1 if total - largest >= number_of - 1 else 0
    holding, rest = [largest] + [least] * (number_of - 1), total - largest - least * (number_of - 1)
    while rest > 0:
        candidates = [i for i in range(1, number_of) if holding[i] < largest] or [i for i in range(1, number_of) if holding[i] < most]
        mass, remaining = sum([loads[i] for i in candidates]), rest
        for i in candidates:
            addition = min(most - holding[i], max(1, remaining * loads[i] // mass), rest)
            holding[i] = holding[i] + addition
            rest = rest - addition
    return np.array(holding)


def gaussian(stream_key, shape, scale, limit, split=(), held_as=jnp.bfloat16):
    level = block_scale(stream_key, shape, split, -0.22, 0.18) if split else 1.0
    result = jax.random.normal(stream_key, shape, jnp.float32) * scale * level
    return jnp.minimum(jnp.maximum(result, -limit), limit).astype(held_as)


def setup_inputs(seed: int = 0) -> dict:
    key_of = jax.random.split(jax.random.key(seed), 11)
    inv_factor = gaussian(key_of[0], (ELEMS, NI, NI), NI ** -0.5, 0.3125, ((0, 32),))
    coupling = gaussian(key_of[1], (ELEMS, NI, NB), 64 ** -0.5, 0.75, ((0, 32),))
    boundary = gaussian(key_of[2], (ELEMS, NB, NB), 1.0, 6.0, ((0, 32),))
    load_int = gaussian(key_of[3], (ELEMS, NI), 1.0, 6.0, ((0, 32),))
    load_bnd = gaussian(key_of[4], (ELEMS, NB), 1.0, 6.0, ((0, 32),))
    counts = ragged_sizes(key_of[5], DEVICES, LIVE * DEVICES, EMAX, 2).astype(jnp.int32)
    tile_owner_keys = jax.random.split(jax.random.fold_in(key_of[6], 1), ELEMS * (TILES * TILES) // ETILES)
    tile_owner_turns = jax.random.permutation(jax.random.fold_in(key_of[6], 3), ELEMS * (TILES * TILES) // ETILES)
    tile_owner = jax.vmap(lambda own, number: deal_out(jax.random.fold_in(key_of[6], 2), own, number, ETILES, DEVICES, 1, CAP, 2))(tile_owner_keys, tile_owner_turns).reshape((ELEMS, TILES * TILES, 1))
    tile_slot = with_ends(jax.random.randint(key_of[7], (ELEMS, TILES * TILES), 0, SLOT_DEV), jax.random.fold_in(key_of[7], 1), 0, SLOT_DEV - 1).astype(jnp.int32)
    vec_owner_keys = jax.random.split(jax.random.fold_in(key_of[8], 1), ELEMS * TILES // (EMAX * TILES))
    vec_owner_turns = jax.random.permutation(jax.random.fold_in(key_of[8], 3), ELEMS * TILES // (EMAX * TILES))
    vec_owner = jax.vmap(lambda own, number: deal_out(jax.random.fold_in(key_of[8], 2), own, number, EMAX * TILES, DEVICES, 1, VCAP, 2))(vec_owner_keys, vec_owner_turns).reshape((ELEMS, TILES, 1))
    vec_slot = with_ends(jax.random.randint(key_of[9], (ELEMS, TILES), 0, VSLOT_DEV), jax.random.fold_in(key_of[9], 1), 0, VSLOT_DEV - 1).astype(jnp.int32)
    return {"inv_factor": inv_factor, "coupling": coupling, "boundary": boundary, "load_int": load_int, "load_bnd": load_bnd, "counts": counts, "tile_owner": tile_owner, "tile_slot": tile_slot, "vec_owner": vec_owner, "vec_slot": vec_slot}


def mult(a, b):
    return jnp.dot(a.astype(jnp.float32), b.astype(jnp.float32), precision=lax.Precision.HIGHEST)


def reference(inv_factor, coupling, boundary, load_int, load_bnd, counts, tile_owner, tile_slot, vec_owner, vec_slot):
    nelem = inv_factor.shape[0]
    nb = boundary.shape[1]
    tiles = nb // BLOCK_UNKNOWNS
    targets = (tile_owner[:, :, 0] * SLOT_DEV + tile_slot).astype(jnp.int32)
    vtargets = (vec_owner[:, :, 0] * VSLOT_DEV + vec_slot).astype(jnp.int32)

    def step(index, carry):
        stiffness_matrices, load_vectors = carry
        elem = jnp.asarray(index).astype(jnp.int32)
        owner_dev = (elem // EMAX).astype(jnp.int32)
        alive = ((elem % EMAX) < lax.dynamic_index_in_dim(counts, owner_dev, 0, keepdims=False)).astype(jnp.float32)
        factor = lax.dynamic_index_in_dim(inv_factor, elem, 0, keepdims=False)
        couple = lax.dynamic_index_in_dim(coupling, elem, 0, keepdims=False)
        bound = lax.dynamic_index_in_dim(boundary, elem, 0, keepdims=False)
        inner = lax.dynamic_index_in_dim(load_int, elem, 0, keepdims=False)
        outer = lax.dynamic_index_in_dim(load_bnd, elem, 0, keepdims=False)
        coupled = mult(factor, couple).astype(jnp.bfloat16)
        schur = (bound.astype(jnp.float32) - mult(coupled.T, coupled)).astype(jnp.bfloat16)
        pulled = mult(factor, inner).astype(jnp.bfloat16)
        condensed = (outer.astype(jnp.float32) - mult(pulled, coupled)).astype(jnp.bfloat16)
        pieces = schur.astype(jnp.float32).reshape(tiles, BLOCK_UNKNOWNS, tiles, BLOCK_UNKNOWNS).transpose(0, 2, 1, 3).reshape(tiles * tiles, BLOCK_UNKNOWNS * BLOCK_UNKNOWNS)
        blocks = condensed.astype(jnp.float32).reshape(tiles, BLOCK_UNKNOWNS)
        rows = lax.dynamic_index_in_dim(targets, elem, 0, keepdims=False)
        vrows = lax.dynamic_index_in_dim(vtargets, elem, 0, keepdims=False)
        stiffness_matrices = stiffness_matrices.at[rows].add(pieces * alive)
        load_vectors = load_vectors.at[vrows].add(blocks * alive)
        return stiffness_matrices, load_vectors

    start_offset = (jnp.zeros((INTERFACE_TILES, BLOCK_UNKNOWNS * BLOCK_UNKNOWNS), jnp.float32), jnp.zeros((LOAD_BLOCK_COUNT, BLOCK_UNKNOWNS), jnp.float32))
    stiffness_matrices, load_vectors = lax.fori_loop(0, nelem, step, start_offset)
    return stiffness_matrices.reshape(INTERFACE_TILES, BLOCK_UNKNOWNS, BLOCK_UNKNOWNS), load_vectors
```

```python
import functools

import jax
import jax.numpy as jnp
from jax import lax
from jax.experimental import pallas as pl
from jax.experimental.pallas import tpu as pltpu
from jax.sharding import PartitionSpec as P

BLOCK_UNKNOWNS = 128
SLOT_DEV = 64
VSLOT_DEV = 16
LANES = 128
MESH = pl.DeviceIdType.MESH


def ranks(owner):
    count = owner.shape[0]
    same = owner[:, None] == owner[None, :]
    before = jnp.arange(count)[None, :] < jnp.arange(count)[:, None]
    return jnp.sum((same & before).astype(jnp.int32), axis=1)


def slot_table(owner, rank, slot, live, peers):
    hit = (owner[None, None, :] == jnp.arange(peers, dtype=jnp.int32)[:, None, None]) & (
        rank[None, None, :] == jnp.arange(LANES, dtype=jnp.int32)[None, :, None]
    )
    return jnp.max(jnp.where(hit & live[None, None, :], slot[None, None, :], -1), axis=2)


def condense_kernel(
    emax,
    tiles,
    counts,
    pos,
    vpos,
    factor_ref,
    couple_ref,
    bound_ref,
    inner_ref,
    outer_ref,
    ids_ref,
    send_ref,
    aux_ref,
    held,
    sems,
):
    tile = BLOCK_UNKNOWNS
    e = pl.program_id(0)
    live = counts[0]
    slot = lax.rem(e, 2)

    def drain(which):
        for t in range(tiles * tiles):
            pltpu.make_async_copy(held.at[which, t], send_ref.at[0], sems.at[which, t]).wait()

    @pl.when(e == 0)
    def _():
        aux_ref[...] = ids_ref[...]

    @pl.when(e < live)
    def _():
        factor = factor_ref[0]
        coupled = jnp.dot(factor, couple_ref[0], preferred_element_type=jnp.float32).astype(
            jnp.bfloat16
        )

        def row(ref):
            whole = ref[...].astype(jnp.float32)
            mine = lax.broadcasted_iota(jnp.int32, whole.shape, 0) == e
            return jnp.sum(jnp.where(mine, whole, 0.0), axis=0, keepdims=True)

        inner = jnp.broadcast_to(row(inner_ref), (8, inner_ref.shape[1])).astype(jnp.bfloat16)
        pulled = lax.dot_general(
            inner, factor, (((1,), (1,)), ((), ())), preferred_element_type=jnp.float32
        ).astype(jnp.bfloat16)
        drop = jnp.dot(pulled, coupled, preferred_element_type=jnp.float32)[0:1]
        condensed = (row(outer_ref) - drop).astype(jnp.bfloat16).astype(jnp.float32)
        for a in range(tiles):
            aux_ref[pl.ds(vpos[e * tiles + a], 1), :] = condensed[:, a * tile : (a + 1) * tile]

        product = lax.dot_general(
            coupled, coupled, (((0,), (0,)), ((), ())), preferred_element_type=jnp.float32
        )

        @pl.when(e >= 2)
        def _():
            drain(slot)

        for a in range(tiles):
            rows = slice(a * tile, (a + 1) * tile)
            for b in range(tiles):
                cols = slice(b * tile, (b + 1) * tile)
                t = a * tiles + b
                held[slot, t] = (
                    bound_ref[0, rows, cols].astype(jnp.float32) - product[rows, cols]
                ).astype(jnp.bfloat16)
                pltpu.make_async_copy(
                    held.at[slot, t],
                    send_ref.at[pos[e * tiles * tiles + t]],
                    sems.at[slot, t],
                ).start()

    @pl.when(e == emax - 1)
    def _():
        @pl.when(live >= 2)
        def _():
            drain(lax.rem(live, 2))

        drain(lax.rem(live + 1, 2))


def exchange_kernel(peers, columns, room, auxrows, send, aux, recv, auxrecv, sems, auxsems, own):
    me = lax.axis_index("grp") * columns + lax.axis_index("blk")

    def coords(d):
        return (d // columns, d % columns)

    barrier = pltpu.get_barrier_semaphore()

    @pl.loop(1, peers)
    def _(k):
        pl.semaphore_signal(
            barrier, inc=1, device_id=coords((me + k) % peers), device_id_type=MESH
        )

    pl.semaphore_wait(barrier, peers - 1)

    def tile_copy(k):
        d = (me + k) % peers
        return pltpu.make_async_remote_copy(
            src_ref=send.at[pl.ds(d * room, room)],
            dst_ref=recv.at[pl.ds(me * room, room)],
            send_sem=sems.at[0, k],
            recv_sem=sems.at[1, k],
            device_id=coords(d),
            device_id_type=MESH,
        )

    def aux_copy(k):
        d = (me + k) % peers
        return pltpu.make_async_remote_copy(
            src_ref=aux.at[pl.ds(d * auxrows, auxrows)],
            dst_ref=auxrecv.at[pl.ds(me * auxrows, auxrows)],
            send_sem=auxsems.at[0, k],
            recv_sem=auxsems.at[1, k],
            device_id=coords(d),
            device_id_type=MESH,
        )

    @pl.loop(1, peers)
    def _(k):
        tile_copy(k).start()
        aux_copy(k).start()

    mine = pltpu.make_async_copy(
        send.at[pl.ds(me * room, room)], recv.at[pl.ds(me * room, room)], own.at[0]
    )
    auxmine = pltpu.make_async_copy(
        aux.at[pl.ds(me * auxrows, auxrows)], auxrecv.at[pl.ds(me * auxrows, auxrows)], own.at[1]
    )
    mine.start()
    auxmine.start()
    mine.wait()
    auxmine.wait()

    @pl.loop(1, peers)
    def _(k):
        tile_copy(k).wait()
        aux_copy(k).wait()


def sum_kernel(
    peers, group, room, vroom, auxrows, ids, vids, recv_ref, aux_ref, out_ref, loads_ref
):
    step = pl.program_id(0)

    @pl.when(step == 0)
    def _():
        out_ref[...] = jnp.zeros_like(out_ref)
        loads_ref[...] = jnp.zeros_like(loads_ref)

        @pl.loop(0, peers)
        def _(p):
            for v in range(vroom):
                target = vids[p * vroom + v]

                @pl.when(target >= 0)
                def _():
                    loads_ref[pl.ds(target, 1), :] += aux_ref[pl.ds(p * auxrows + v, 1), :]

    @pl.loop(0, group * room)
    def _(t):
        target = ids[step * group * room + t]

        @pl.when(target >= 0)
        def _():
            out_ref[target] += recv_ref[t].astype(jnp.float32)


def shards(
    inv_factor,
    coupling,
    boundary,
    load_int,
    load_bnd,
    counts,
    tile_owner,
    tile_slot,
    vec_owner,
    vec_slot,
):
    emax, ni, _ = inv_factor.shape
    nb = boundary.shape[1]
    tile = BLOCK_UNKNOWNS
    tiles = nb // tile
    columns = lax.axis_size("blk")
    peers = lax.axis_size("grp") * columns
    ntiles = emax * tiles * tiles
    room = max(2, 3 * ntiles // (2 * peers))
    vroom = max(2, 3 * emax * tiles // (2 * peers))
    vrows = -(-vroom // 8) * 8
    auxrows = vrows + 8

    owner = tile_owner.reshape(-1)
    vowner = vec_owner.reshape(-1)
    rank, vrank = ranks(owner), ranks(vowner)
    pos = owner * room + rank
    vpos = vowner * auxrows + vrank
    live = jnp.arange(ntiles) < counts[0] * (tiles * tiles)
    vlive = jnp.arange(emax * tiles) < counts[0] * tiles
    ids = slot_table(owner, rank, tile_slot.reshape(-1), live, peers)
    vids = slot_table(vowner, vrank, vec_slot.reshape(-1), vlive, peers)
    at = lax.broadcasted_iota(jnp.int32, (1, auxrows, 1), 1)
    table = jnp.where(
        at == vrows, ids[:, None, :], jnp.where(at == vrows + 1, vids[:, None, :], 0)
    )
    table = table.astype(jnp.float32).reshape(peers * auxrows, LANES)

    def element(e, cnt, *_):
        return (jnp.minimum(e, cnt[0] - 1), 0, 0)

    def whole(*_):
        return (0, 0)

    send, aux = pl.pallas_call(
        functools.partial(condense_kernel, emax, tiles),
        grid_spec=pltpu.PrefetchScalarGridSpec(
            num_scalar_prefetch=3,
            grid=(emax,),
            in_specs=[
                pl.BlockSpec((1, ni, ni), element),
                pl.BlockSpec((1, ni, nb), element),
                pl.BlockSpec((1, nb, nb), element),
                pl.BlockSpec((emax, ni), whole),
                pl.BlockSpec((emax, nb), whole),
                pl.BlockSpec((peers * auxrows, LANES), whole),
            ],
            out_specs=[
                pl.BlockSpec(memory_space=pl.ANY),
                pl.BlockSpec((peers * auxrows, LANES), whole),
            ],
            scratch_shapes=[
                pltpu.VMEM((2, tiles * tiles, tile, tile), jnp.bfloat16),
                pltpu.SemaphoreType.DMA((2, tiles * tiles)),
            ],
        ),
        out_shape=[
            jax.ShapeDtypeStruct((peers * room, tile, tile), jnp.bfloat16),
            jax.ShapeDtypeStruct((peers * auxrows, LANES), jnp.float32),
        ],
        compiler_params=pltpu.CompilerParams(
            dimension_semantics=("arbitrary",), vmem_limit_bytes=40 * 1024 * 1024
        ),
        name="condense",
    )(counts, pos, vpos, inv_factor, coupling, boundary, load_int, load_bnd, table)

    recv, auxrecv = pl.pallas_call(
        functools.partial(exchange_kernel, peers, columns, room, auxrows),
        in_specs=[pl.BlockSpec(memory_space=pl.ANY)] * 2,
        out_specs=[pl.BlockSpec(memory_space=pl.ANY)] * 2,
        out_shape=[
            jax.ShapeDtypeStruct((peers * room, tile, tile), jnp.bfloat16),
            jax.ShapeDtypeStruct((peers * auxrows, LANES), jnp.float32),
        ],
        scratch_shapes=[
            pltpu.SemaphoreType.DMA((2, peers)),
            pltpu.SemaphoreType.DMA((2, peers)),
            pltpu.SemaphoreType.DMA((2,)),
        ],
        compiler_params=pltpu.CompilerParams(collective_id=0, has_side_effects=True),
        name="exchange",
    )(send, aux)

    got = auxrecv.reshape(peers, auxrows, LANES)
    got_ids = got[:, vrows, :room].astype(jnp.int32).reshape(-1)
    got_vids = got[:, vrows + 1, :vroom].astype(jnp.int32).reshape(-1)
    group = 4 if peers % 4 == 0 else 1

    assembled, loads = pl.pallas_call(
        functools.partial(sum_kernel, peers, group, room, vroom, auxrows),
        grid_spec=pltpu.PrefetchScalarGridSpec(
            num_scalar_prefetch=2,
            grid=(peers // group,),
            in_specs=[
                pl.BlockSpec((group * room, tile, tile), lambda s, *_: (s, 0, 0)),
                pl.BlockSpec((peers * auxrows, LANES), whole),
            ],
            out_specs=[
                pl.BlockSpec((SLOT_DEV, tile, tile), lambda s, *_: (0, 0, 0)),
                pl.BlockSpec((VSLOT_DEV, LANES), whole),
            ],
        ),
        out_shape=[
            jax.ShapeDtypeStruct((SLOT_DEV, tile, tile), jnp.float32),
            jax.ShapeDtypeStruct((VSLOT_DEV, LANES), jnp.float32),
        ],
        compiler_params=pltpu.CompilerParams(
            dimension_semantics=("arbitrary",), vmem_limit_bytes=40 * 1024 * 1024
        ),
        name="assemble",
    )(got_ids, got_vids, recv, auxrecv)
    return (assembled, loads)


def solution(mesh):
    in_specs = (
        P(("grp", "blk"), None, None),
        P(("grp", "blk"), None, None),
        P(("grp", "blk"), None, None),
        P(("grp", "blk"), None),
        P(("grp", "blk"), None),
        P(("grp", "blk")),
        P(("grp", "blk"), None, None),
        P(("grp", "blk"), None),
        P(("grp", "blk"), None, None),
        P(("grp", "blk"), None),
    )
    out_specs = (P(("grp", "blk"), None, None), P(("grp", "blk"), None))
    return jax.shard_map(shards, mesh=mesh, in_specs=in_specs, out_specs=out_specs, check_vma=False)
```

```python
import functools

import jax
import jax.numpy as jnp
from jax import lax
from jax.experimental import pallas as pl
from jax.experimental.pallas import tpu as pltpu
from jax.sharding import PartitionSpec as P

BLOCK_UNKNOWNS = 128
SLOT_DEV = 64
VSLOT_DEV = 16
LANES = 128
DIRECT = 80
VMEM_LIMIT = 58 * 1024 * 1024
MESH = pl.DeviceIdType.MESH


def ranks(owner):
    count = owner.shape[0]
    same = owner[:, None] == owner[None, :]
    before = jnp.arange(count)[None, :] < jnp.arange(count)[:, None]
    return jnp.sum((same & before).astype(jnp.int32), axis=1)


def slot_table(owner, rank, slot, live, peers):
    hit = (owner[None, None, :] == jnp.arange(peers, dtype=jnp.int32)[:, None, None]) & (
        rank[None, None, :] == jnp.arange(LANES, dtype=jnp.int32)[None, :, None]
    )
    return jnp.max(jnp.where(hit & live[None, None, :], slot[None, None, :], -1), axis=2)


def condense_kernel(
    emax,
    tiles,
    counts,
    pos,
    vpos,
    factor_ref,
    couple_ref,
    bound_ref,
    inner_ref,
    outer_ref,
    ids_ref,
    send_ref,
    aux_ref,
    held,
    sems,
):
    tile = BLOCK_UNKNOWNS
    e = pl.program_id(0)
    live = counts[0]
    slot = lax.rem(e, 2)

    def drain(which):
        for t in range(tiles * tiles):
            pltpu.make_async_copy(held.at[which, t], send_ref.at[0], sems.at[which, t]).wait()

    @pl.when(e == 0)
    def _():
        aux_ref[...] = ids_ref[...]

    @pl.when(e < live)
    def _():
        factor = factor_ref[0]
        coupled = jnp.dot(factor, couple_ref[0], preferred_element_type=jnp.float32).astype(
            jnp.bfloat16
        )

        def row(ref):
            whole = ref[...].astype(jnp.float32)
            mine = lax.broadcasted_iota(jnp.int32, whole.shape, 0) == e
            return jnp.sum(jnp.where(mine, whole, 0.0), axis=0, keepdims=True)

        inner = jnp.broadcast_to(row(inner_ref), (8, inner_ref.shape[1])).astype(jnp.bfloat16)
        pulled = lax.dot_general(
            inner, factor, (((1,), (1,)), ((), ())), preferred_element_type=jnp.float32
        ).astype(jnp.bfloat16)
        drop = jnp.dot(pulled, coupled, preferred_element_type=jnp.float32)[0:1]
        condensed = (row(outer_ref) - drop).astype(jnp.bfloat16).astype(jnp.float32)
        for a in range(tiles):
            aux_ref[pl.ds(vpos[e * tiles + a], 1), :] = condensed[:, a * tile : (a + 1) * tile]

        product = lax.dot_general(
            coupled, coupled, (((0,), (0,)), ((), ())), preferred_element_type=jnp.float32
        )

        @pl.when(e >= 2)
        def _():
            drain(slot)

        for a in range(tiles):
            rows = slice(a * tile, (a + 1) * tile)
            for b in range(tiles):
                cols = slice(b * tile, (b + 1) * tile)
                t = a * tiles + b
                held[slot, t] = (
                    bound_ref[0, rows, cols].astype(jnp.float32) - product[rows, cols]
                ).astype(jnp.bfloat16)
                pltpu.make_async_copy(
                    held.at[slot, t],
                    send_ref.at[pos[e * tiles * tiles + t]],
                    sems.at[slot, t],
                ).start()

    @pl.when(e == emax - 1)
    def _():
        @pl.when(live >= 2)
        def _():
            drain(lax.rem(live, 2))

        drain(lax.rem(live + 1, 2))


def exchange_kernel(
    groups,
    columns,
    room,
    vrows,
    auxrows,
    direct,
    send,
    aux,
    recv,
    relay,
    auxrecv,
    auxrelay,
    sems,
    auxsems,
    own,
):
    peers = groups * columns
    part = columns // 2
    half = peers // 2
    tile = BLOCK_UNKNOWNS
    g, c = lax.axis_index("grp"), lax.axis_index("blk")
    me = g * columns + c
    base = (c // part) * part
    inner = c % part
    mine = g * part + inner

    def near(j):
        return (g + j // part) % groups, base + (inner + j % part) % part

    def far(j):
        return (g + j // part) % groups, (part - base) + (inner + j % part) % part

    barrier = pltpu.get_barrier_semaphore()

    @pl.loop(1, peers)
    def _(k):
        d = (me + k) % peers
        pl.semaphore_signal(
            barrier, inc=1, device_id=(d // columns, d % columns), device_id_type=MESH
        )

    pl.semaphore_wait(barrier, peers - 1)

    def remote(src, dst, table, kind, j, device):
        return pltpu.make_async_remote_copy(
            src_ref=src,
            dst_ref=dst,
            send_sem=table.at[2 * kind, j],
            recv_sem=table.at[2 * kind + 1, j],
            device_id=device,
            device_id_type=MESH,
        )

    def flat(device):
        return device[0] * columns + device[1]

    def near_copies(j):
        device = near(j)
        d = flat(device)
        return (
            remote(
                send.at[pl.ds(d * room, room)],
                recv.at[pl.ds(me * room, room)],
                sems, 0, j, device,
            ),
            remote(
                aux.at[pl.ds(d * auxrows, auxrows)],
                auxrecv.at[pl.ds(me * auxrows, auxrows)],
                auxsems, 0, j, device,
            ),
        )

    def far_copies(j):
        device = far(j)
        d = flat(device)
        return (
            remote(
                send.at[pl.ds(d * room, room), pl.ds(0, direct)],
                recv.at[pl.ds(me * room, room), pl.ds(0, direct)],
                sems, 1, j, device,
            ),
            remote(
                aux.at[pl.ds(d * auxrows, auxrows)],
                auxrecv.at[pl.ds(me * auxrows, auxrows)],
                auxsems, 1, j, device,
            ),
        )

    def relay_copies(j):
        device = near(j)
        d = flat(far(j))
        return (
            remote(
                send.at[pl.ds(d * room, room), pl.ds(direct, tile - direct)],
                relay.at[pl.ds(mine * room, room)],
                sems, 2, j, device,
            ),
            remote(
                aux.at[pl.ds(d * auxrows + vrows, 8)],
                auxrelay.at[pl.ds(mine * 8, 8)],
                auxsems, 2, j, device,
            ),
        )

    for copy in far_copies(0):
        copy.start()

    @pl.loop(1, half)
    def _(j):
        for copy in far_copies(j) + relay_copies(j) + near_copies(j):
            copy.start()

    twin = flat(far(0))
    local = (
        pltpu.make_async_copy(
            send.at[pl.ds(me * room, room)], recv.at[pl.ds(me * room, room)], own.at[0]
        ),
        pltpu.make_async_copy(
            aux.at[pl.ds(me * auxrows, auxrows)],
            auxrecv.at[pl.ds(me * auxrows, auxrows)],
            own.at[1],
        ),
        pltpu.make_async_copy(
            send.at[pl.ds(twin * room, room), pl.ds(direct, tile - direct)],
            relay.at[pl.ds(mine * room, room)],
            own.at[2],
        ),
        pltpu.make_async_copy(
            aux.at[pl.ds(twin * auxrows + vrows, 8)], auxrelay.at[pl.ds(mine * 8, 8)], own.at[3]
        ),
    )
    for copy in local:
        copy.start()
    for copy in local:
        copy.wait()
    for copy in far_copies(0):
        copy.wait()

    @pl.loop(1, half)
    def _(j):
        for copy in far_copies(j) + relay_copies(j) + near_copies(j):
            copy.wait()


def relay_kernel(group, room, ids, relay_ref, out_ref, total):
    step = pl.program_id(0)

    @pl.when(step == 0)
    def _():
        total[...] = jnp.zeros_like(total)

    @pl.loop(0, group * room)
    def _(t):
        target = ids[step * group * room + t]

        @pl.when(target >= 0)
        def _():
            total[target] += relay_ref[t].astype(jnp.float32)

    @pl.when(step == pl.num_programs(0) - 1)
    def _():
        out_ref[...] = total[...].astype(out_ref.dtype)


def swap_kernel(columns, mine, other, sems):
    part = columns // 2
    g, c = lax.axis_index("grp"), lax.axis_index("blk")
    twin = (g, (c + part) % columns)
    barrier = pltpu.get_barrier_semaphore()
    pl.semaphore_signal(barrier, inc=1, device_id=twin, device_id_type=MESH)
    pl.semaphore_wait(barrier, 1)
    copy = pltpu.make_async_remote_copy(
        src_ref=mine,
        dst_ref=other,
        send_sem=sems.at[0],
        recv_sem=sems.at[1],
        device_id=twin,
        device_id_type=MESH,
    )
    copy.start()
    copy.wait()


def sum_kernel(
    peers,
    group,
    room,
    vroom,
    auxrows,
    direct,
    ids,
    vids,
    close,
    recv_ref,
    aux_ref,
    far_ref,
    out_ref,
    loads_ref,
):
    step = pl.program_id(0)
    tile = BLOCK_UNKNOWNS

    @pl.when(step == 0)
    def _():
        out_ref[:, :direct, :] = jnp.zeros((SLOT_DEV, direct, tile), jnp.float32)
        out_ref[:, direct:, :] = far_ref[...].astype(jnp.float32)
        loads_ref[...] = jnp.zeros_like(loads_ref)

        @pl.loop(0, peers)
        def _(p):
            for v in range(vroom):
                target = vids[p * vroom + v]

                @pl.when(target >= 0)
                def _():
                    loads_ref[pl.ds(target, 1), :] += aux_ref[pl.ds(p * auxrows + v, 1), :]

    for p in range(group):
        whole = close[step * group + p] > 0

        @pl.loop(0, room)
        def _(r):
            t = p * room + r
            target = ids[step * group * room + t]

            @pl.when((target >= 0) & whole)
            def _():
                out_ref[target] += recv_ref[t].astype(jnp.float32)

            @pl.when((target >= 0) & jnp.logical_not(whole))
            def _():
                out_ref[target, :direct, :] += recv_ref[t, :direct, :].astype(jnp.float32)


def shards(
    inv_factor,
    coupling,
    boundary,
    load_int,
    load_bnd,
    counts,
    tile_owner,
    tile_slot,
    vec_owner,
    vec_slot,
):
    emax, ni, _ = inv_factor.shape
    nb = boundary.shape[1]
    tile = BLOCK_UNKNOWNS
    tiles = nb // tile
    columns = lax.axis_size("blk")
    peers = lax.axis_size("grp") * columns
    ntiles = emax * tiles * tiles
    room = max(2, 3 * ntiles // (2 * peers))
    vroom = max(2, 3 * emax * tiles // (2 * peers))
    vrows = -(-vroom // 8) * 8
    auxrows = vrows + 8

    owner = tile_owner.reshape(-1)
    vowner = vec_owner.reshape(-1)
    rank, vrank = ranks(owner), ranks(vowner)
    pos = owner * room + rank
    vpos = vowner * auxrows + vrank
    live = jnp.arange(ntiles) < counts[0] * (tiles * tiles)
    vlive = jnp.arange(emax * tiles) < counts[0] * tiles
    ids = slot_table(owner, rank, tile_slot.reshape(-1), live, peers)
    vids = slot_table(vowner, vrank, vec_slot.reshape(-1), vlive, peers)
    at = lax.broadcasted_iota(jnp.int32, (1, auxrows, 1), 1)
    table = jnp.where(
        at == vrows, ids[:, None, :], jnp.where(at == vrows + 1, vids[:, None, :], 0)
    )
    table = table.astype(jnp.float32).reshape(peers * auxrows, LANES)

    def element(e, cnt, *_):
        return (jnp.minimum(e, cnt[0] - 1), 0, 0)

    def whole(*_):
        return (0, 0)

    send, aux = pl.pallas_call(
        functools.partial(condense_kernel, emax, tiles),
        grid_spec=pltpu.PrefetchScalarGridSpec(
            num_scalar_prefetch=3,
            grid=(emax,),
            in_specs=[
                pl.BlockSpec((1, ni, ni), element),
                pl.BlockSpec((1, ni, nb), element),
                pl.BlockSpec((1, nb, nb), element),
                pl.BlockSpec((emax, ni), whole),
                pl.BlockSpec((emax, nb), whole),
                pl.BlockSpec((peers * auxrows, LANES), whole),
            ],
            out_specs=[
                pl.BlockSpec(memory_space=pl.ANY),
                pl.BlockSpec((peers * auxrows, LANES), whole),
            ],
            scratch_shapes=[
                pltpu.VMEM((2, tiles * tiles, tile, tile), jnp.bfloat16),
                pltpu.SemaphoreType.DMA((2, tiles * tiles)),
            ],
        ),
        out_shape=[
            jax.ShapeDtypeStruct((peers * room, tile, tile), jnp.bfloat16),
            jax.ShapeDtypeStruct((peers * auxrows, LANES), jnp.float32),
        ],
        compiler_params=pltpu.CompilerParams(
            dimension_semantics=("arbitrary",), vmem_limit_bytes=VMEM_LIMIT
        ),
        name="condense",
    )(counts, pos, vpos, inv_factor, coupling, boundary, load_int, load_bnd, table)

    half = peers // 2
    recv, relay, auxrecv, auxrelay = pl.pallas_call(
        functools.partial(
            exchange_kernel, peers // columns, columns, room, vrows, auxrows, DIRECT
        ),
        in_specs=[pl.BlockSpec(memory_space=pl.ANY)] * 2,
        out_specs=[pl.BlockSpec(memory_space=pl.ANY)] * 4,
        out_shape=[
            jax.ShapeDtypeStruct((peers * room, tile, tile), jnp.bfloat16),
            jax.ShapeDtypeStruct((half * room, tile - DIRECT, tile), jnp.bfloat16),
            jax.ShapeDtypeStruct((peers * auxrows, LANES), jnp.float32),
            jax.ShapeDtypeStruct((half * 8, LANES), jnp.float32),
        ],
        scratch_shapes=[
            pltpu.SemaphoreType.DMA((6, half)),
            pltpu.SemaphoreType.DMA((6, half)),
            pltpu.SemaphoreType.DMA((4,)),
        ],
        compiler_params=pltpu.CompilerParams(
            collective_id=0, has_side_effects=True, vmem_limit_bytes=VMEM_LIMIT
        ),
        name="exchange",
    )(send, aux)

    relay_ids = auxrelay.reshape(half, 8, LANES)[:, 0, :room].astype(jnp.int32).reshape(-1)
    group = 4 if half % 4 == 0 else 1
    partial = pl.pallas_call(
        functools.partial(relay_kernel, group, room),
        grid_spec=pltpu.PrefetchScalarGridSpec(
            num_scalar_prefetch=1,
            grid=(half // group,),
            in_specs=[
                pl.BlockSpec((group * room, tile - DIRECT, tile), lambda s, *_: (s, 0, 0)),
            ],
            out_specs=pl.BlockSpec((SLOT_DEV, tile - DIRECT, tile), lambda s, *_: (0, 0, 0)),
            scratch_shapes=[pltpu.VMEM((SLOT_DEV, tile - DIRECT, tile), jnp.float32)],
        ),
        out_shape=jax.ShapeDtypeStruct((SLOT_DEV, tile - DIRECT, tile), jnp.bfloat16),
        compiler_params=pltpu.CompilerParams(
            dimension_semantics=("arbitrary",), vmem_limit_bytes=VMEM_LIMIT
        ),
        name="relay",
    )(relay_ids, relay)

    other = pl.pallas_call(
        functools.partial(swap_kernel, columns),
        in_specs=[pl.BlockSpec(memory_space=pl.ANY)],
        out_specs=pl.BlockSpec(memory_space=pl.ANY),
        out_shape=jax.ShapeDtypeStruct(partial.shape, jnp.bfloat16),
        scratch_shapes=[pltpu.SemaphoreType.DMA((2,))],
        compiler_params=pltpu.CompilerParams(
            collective_id=1, has_side_effects=True, vmem_limit_bytes=VMEM_LIMIT
        ),
        name="swap",
    )(partial)

    got = auxrecv.reshape(peers, auxrows, LANES)
    got_ids = got[:, vrows, :room].astype(jnp.int32).reshape(-1)
    got_vids = got[:, vrows + 1, :vroom].astype(jnp.int32).reshape(-1)
    part = columns // 2
    source = jnp.arange(peers, dtype=jnp.int32) % columns
    close = (source // part == lax.axis_index("blk") // part).astype(jnp.int32)

    assembled, loads = pl.pallas_call(
        functools.partial(sum_kernel, peers, group, room, vroom, auxrows, DIRECT),
        grid_spec=pltpu.PrefetchScalarGridSpec(
            num_scalar_prefetch=3,
            grid=(peers // group,),
            in_specs=[
                pl.BlockSpec((group * room, tile, tile), lambda s, *_: (s, 0, 0)),
                pl.BlockSpec((peers * auxrows, LANES), whole),
                pl.BlockSpec((SLOT_DEV, tile - DIRECT, tile), lambda s, *_: (0, 0, 0)),
            ],
            out_specs=[
                pl.BlockSpec((SLOT_DEV, tile, tile), lambda s, *_: (0, 0, 0)),
                pl.BlockSpec((VSLOT_DEV, LANES), whole),
            ],
        ),
        out_shape=[
            jax.ShapeDtypeStruct((SLOT_DEV, tile, tile), jnp.float32),
            jax.ShapeDtypeStruct((VSLOT_DEV, LANES), jnp.float32),
        ],
        compiler_params=pltpu.CompilerParams(
            dimension_semantics=("arbitrary",), vmem_limit_bytes=VMEM_LIMIT
        ),
        name="assemble",
    )(got_ids, got_vids, close, recv, auxrecv, other)
    return (assembled, loads)


def solution(mesh):
    in_specs = (
        P(("grp", "blk"), None, None),
        P(("grp", "blk"), None, None),
        P(("grp", "blk"), None, None),
        P(("grp", "blk"), None),
        P(("grp", "blk"), None),
        P(("grp", "blk")),
        P(("grp", "blk"), None, None),
        P(("grp", "blk"), None),
        P(("grp", "blk"), None, None),
        P(("grp", "blk"), None),
    )
    out_specs = (P(("grp", "blk"), None, None), P(("grp", "blk"), None))
    return jax.shard_map(shards, mesh=mesh, in_specs=in_specs, out_specs=out_specs, check_vma=False)
```

```python
import functools

import jax
import jax.numpy as jnp
from jax import lax
from jax.experimental import pallas as pl
from jax.experimental.pallas import tpu as pltpu
from jax.sharding import PartitionSpec as P

BLOCK_UNKNOWNS = 128
SLOT_DEV = 64
VSLOT_DEV = 16
LANES = 128
DIRECT = 80
VMEM_LIMIT = 58 * 1024 * 1024
MESH = pl.DeviceIdType.MESH


def ranks(owner):
    count = owner.shape[0]
    same = owner[:, None] == owner[None, :]
    before = jnp.arange(count)[None, :] < jnp.arange(count)[:, None]
    return jnp.sum((same & before).astype(jnp.int32), axis=1)


def slot_table(owner, rank, slot, live, peers):
    hit = (owner[None, None, :] == jnp.arange(peers, dtype=jnp.int32)[:, None, None]) & (
        rank[None, None, :] == jnp.arange(LANES, dtype=jnp.int32)[None, :, None]
    )
    return jnp.max(jnp.where(hit & live[None, None, :], slot[None, None, :], -1), axis=2)


def condense_kernel(
    emax,
    tiles,
    counts,
    pos,
    vpos,
    factor_ref,
    couple_ref,
    bound_ref,
    inner_ref,
    outer_ref,
    ids_ref,
    send_ref,
    aux_ref,
    held,
    sems,
):
    tile = BLOCK_UNKNOWNS
    e = pl.program_id(0)
    live = counts[0]
    slot = lax.rem(e, 2)

    def drain(which):
        for t in range(tiles * tiles):
            pltpu.make_async_copy(held.at[which, t], send_ref.at[0], sems.at[which, t]).wait()

    @pl.when(e == 0)
    def _():
        aux_ref[...] = ids_ref[...]

    @pl.when(e < live)
    def _():
        factor = factor_ref[0]
        coupled = jnp.dot(factor, couple_ref[0], preferred_element_type=jnp.float32).astype(
            jnp.bfloat16
        )

        def row(ref):
            whole = ref[...].astype(jnp.float32)
            mine = lax.broadcasted_iota(jnp.int32, whole.shape, 0) == e
            return jnp.sum(jnp.where(mine, whole, 0.0), axis=0, keepdims=True)

        inner = jnp.broadcast_to(row(inner_ref), (8, inner_ref.shape[1])).astype(jnp.bfloat16)
        pulled = lax.dot_general(
            inner, factor, (((1,), (1,)), ((), ())), preferred_element_type=jnp.float32
        ).astype(jnp.bfloat16)
        drop = jnp.dot(pulled, coupled, preferred_element_type=jnp.float32)[0:1]
        condensed = (row(outer_ref) - drop).astype(jnp.bfloat16).astype(jnp.float32)
        for a in range(tiles):
            aux_ref[pl.ds(vpos[e * tiles + a], 1), :] = condensed[:, a * tile : (a + 1) * tile]

        product = lax.dot_general(
            coupled, coupled, (((0,), (0,)), ((), ())), preferred_element_type=jnp.float32
        )

        @pl.when(e >= 2)
        def _():
            drain(slot)

        for a in range(tiles):
            rows = slice(a * tile, (a + 1) * tile)
            for b in range(tiles):
                cols = slice(b * tile, (b + 1) * tile)
                t = a * tiles + b
                held[slot, t] = (
                    bound_ref[0, rows, cols].astype(jnp.float32) - product[rows, cols]
                ).astype(jnp.bfloat16)
                pltpu.make_async_copy(
                    held.at[slot, t],
                    send_ref.at[pos[e * tiles * tiles + t]],
                    sems.at[slot, t],
                ).start()

    @pl.when(e == emax - 1)
    def _():
        @pl.when(live >= 2)
        def _():
            drain(lax.rem(live, 2))

        drain(lax.rem(live + 1, 2))


def exchange_kernel(
    groups,
    columns,
    room,
    vrows,
    auxrows,
    direct,
    send,
    aux,
    recv,
    relay,
    auxrecv,
    auxrelay,
    sems,
    auxsems,
    own,
):
    peers = groups * columns
    part = columns // 2
    half = peers // 2
    tile = BLOCK_UNKNOWNS
    g, c = lax.axis_index("grp"), lax.axis_index("blk")
    me = g * columns + c
    base = (c // part) * part
    inner = c % part
    mine = g * part + inner

    def near(j):
        return (g + j // part) % groups, base + (inner + j % part) % part

    def far(j):
        return (g + j // part) % groups, (part - base) + (inner + j % part) % part

    barrier = pltpu.get_barrier_semaphore()

    @pl.loop(1, peers)
    def _(k):
        d = (me + k) % peers
        pl.semaphore_signal(
            barrier, inc=1, device_id=(d // columns, d % columns), device_id_type=MESH
        )

    pl.semaphore_wait(barrier, peers - 1)

    def remote(src, dst, table, kind, j, device):
        return pltpu.make_async_remote_copy(
            src_ref=src,
            dst_ref=dst,
            send_sem=table.at[2 * kind, j],
            recv_sem=table.at[2 * kind + 1, j],
            device_id=device,
            device_id_type=MESH,
        )

    def flat(device):
        return device[0] * columns + device[1]

    def near_copies(j):
        device = near(j)
        d = flat(device)
        return (
            remote(
                send.at[pl.ds(d * room, room)],
                recv.at[pl.ds(me * room, room)],
                sems, 0, j, device,
            ),
            remote(
                aux.at[pl.ds(d * auxrows, auxrows)],
                auxrecv.at[pl.ds(me * auxrows, auxrows)],
                auxsems, 0, j, device,
            ),
        )

    def far_copies(j):
        device = far(j)
        d = flat(device)
        return (
            remote(
                send.at[pl.ds(d * room, room), pl.ds(0, direct)],
                recv.at[pl.ds(me * room, room), pl.ds(0, direct)],
                sems, 1, j, device,
            ),
            remote(
                aux.at[pl.ds(d * auxrows, auxrows)],
                auxrecv.at[pl.ds(me * auxrows, auxrows)],
                auxsems, 1, j, device,
            ),
        )

    def relay_copies(j):
        device = near(j)
        d = flat(far(j))
        return (
            remote(
                send.at[pl.ds(d * room, room), pl.ds(direct, tile - direct)],
                relay.at[pl.ds(mine * room, room)],
                sems, 2, j, device,
            ),
            remote(
                aux.at[pl.ds(d * auxrows + vrows, 8)],
                auxrelay.at[pl.ds(mine * 8, 8)],
                auxsems, 2, j, device,
            ),
        )

    for copy in far_copies(0):
        copy.start()

    @pl.loop(1, half)
    def _(j):
        for copy in far_copies(j) + relay_copies(j) + near_copies(j):
            copy.start()

    twin = flat(far(0))
    local = (
        pltpu.make_async_copy(
            send.at[pl.ds(me * room, room)], recv.at[pl.ds(me * room, room)], own.at[0]
        ),
        pltpu.make_async_copy(
            aux.at[pl.ds(me * auxrows, auxrows)],
            auxrecv.at[pl.ds(me * auxrows, auxrows)],
            own.at[1],
        ),
        pltpu.make_async_copy(
            send.at[pl.ds(twin * room, room), pl.ds(direct, tile - direct)],
            relay.at[pl.ds(mine * room, room)],
            own.at[2],
        ),
        pltpu.make_async_copy(
            aux.at[pl.ds(twin * auxrows + vrows, 8)], auxrelay.at[pl.ds(mine * 8, 8)], own.at[3]
        ),
    )
    for copy in local:
        copy.start()
    for copy in local:
        copy.wait()
    for copy in far_copies(0):
        copy.wait()

    @pl.loop(1, half)
    def _(j):
        for copy in far_copies(j) + relay_copies(j) + near_copies(j):
            copy.wait()


def relay_kernel(group, room, ids, relay_ref, out_ref, total):
    step = pl.program_id(0)

    @pl.when(step == 0)
    def _():
        total[...] = jnp.zeros_like(total)

    for p in range(group):

        @pl.loop(0, room)
        def _(r):
            target = ids[p * 8, r].astype(jnp.int32)

            @pl.when(target >= 0)
            def _():
                total[target] += relay_ref[p * room + r].astype(jnp.float32)

    @pl.when(step == pl.num_programs(0) - 1)
    def _():
        out_ref[...] = total[...].astype(out_ref.dtype)


def sum_kernel(
    group, room, vroom, vrows, direct, close, ids, recv_ref, aux_ref, out_ref, loads_ref
):
    step = pl.program_id(0)
    auxrows = vrows + 8

    @pl.when(step == 0)
    def _():
        out_ref[...] = jnp.zeros_like(out_ref)
        loads_ref[...] = jnp.zeros_like(loads_ref)

    for p in range(group):
        first = p * auxrows
        whole = close[step * group + p] > 0

        for v in range(vroom):
            slot = ids[first + vrows + 1, v].astype(jnp.int32)

            @pl.when(slot >= 0)
            def _():
                loads_ref[pl.ds(slot, 1), :] += aux_ref[pl.ds(first + v, 1), :]

        @pl.when(whole)
        def _():
            @pl.loop(0, room)
            def _(r):
                target = ids[first + vrows, r].astype(jnp.int32)

                @pl.when(target >= 0)
                def _():
                    out_ref[target] += recv_ref[p * room + r].astype(jnp.float32)

        @pl.when(jnp.logical_not(whole))
        def _():
            @pl.loop(0, room)
            def _(r):
                target = ids[first + vrows, r].astype(jnp.int32)

                @pl.when(target >= 0)
                def _():
                    out_ref[target, :direct, :] += recv_ref[p * room + r, :direct, :].astype(
                        jnp.float32
                    )


def add_kernel(sum_ref, far_ref, out_ref):
    out_ref[...] = sum_ref[...] + far_ref[...].astype(jnp.float32)


def shards(
    inv_factor,
    coupling,
    boundary,
    load_int,
    load_bnd,
    counts,
    tile_owner,
    tile_slot,
    vec_owner,
    vec_slot,
):
    emax, ni, _ = inv_factor.shape
    nb = boundary.shape[1]
    tile = BLOCK_UNKNOWNS
    tiles = nb // tile
    columns = lax.axis_size("blk")
    peers = lax.axis_size("grp") * columns
    ntiles = emax * tiles * tiles
    room = max(2, 3 * ntiles // (2 * peers))
    vroom = max(2, 3 * emax * tiles // (2 * peers))
    vrows = -(-vroom // 8) * 8
    auxrows = vrows + 8

    owner = tile_owner.reshape(-1)
    vowner = vec_owner.reshape(-1)
    rank, vrank = ranks(owner), ranks(vowner)
    pos = owner * room + rank
    vpos = vowner * auxrows + vrank
    live = jnp.arange(ntiles) < counts[0] * (tiles * tiles)
    vlive = jnp.arange(emax * tiles) < counts[0] * tiles
    ids = slot_table(owner, rank, tile_slot.reshape(-1), live, peers)
    vids = slot_table(vowner, vrank, vec_slot.reshape(-1), vlive, peers)
    at = lax.broadcasted_iota(jnp.int32, (1, auxrows, 1), 1)
    table = jnp.where(
        at == vrows, ids[:, None, :], jnp.where(at == vrows + 1, vids[:, None, :], 0)
    )
    table = table.astype(jnp.float32).reshape(peers * auxrows, LANES)

    def element(e, cnt, *_):
        return (jnp.minimum(e, cnt[0] - 1), 0, 0)

    def whole(*_):
        return (0, 0)

    send, aux = pl.pallas_call(
        functools.partial(condense_kernel, emax, tiles),
        grid_spec=pltpu.PrefetchScalarGridSpec(
            num_scalar_prefetch=3,
            grid=(emax,),
            in_specs=[
                pl.BlockSpec((1, ni, ni), element),
                pl.BlockSpec((1, ni, nb), element),
                pl.BlockSpec((1, nb, nb), element),
                pl.BlockSpec((emax, ni), whole),
                pl.BlockSpec((emax, nb), whole),
                pl.BlockSpec((peers * auxrows, LANES), whole),
            ],
            out_specs=[
                pl.BlockSpec(memory_space=pl.ANY),
                pl.BlockSpec((peers * auxrows, LANES), whole),
            ],
            scratch_shapes=[
                pltpu.VMEM((2, tiles * tiles, tile, tile), jnp.bfloat16),
                pltpu.SemaphoreType.DMA((2, tiles * tiles)),
            ],
        ),
        out_shape=[
            jax.ShapeDtypeStruct((peers * room, tile, tile), jnp.bfloat16),
            jax.ShapeDtypeStruct((peers * auxrows, LANES), jnp.float32),
        ],
        compiler_params=pltpu.CompilerParams(
            dimension_semantics=("arbitrary",), vmem_limit_bytes=VMEM_LIMIT
        ),
        name="condense",
    )(counts, pos, vpos, inv_factor, coupling, boundary, load_int, load_bnd, table)

    half = peers // 2
    recv, relay, auxrecv, auxrelay = pl.pallas_call(
        functools.partial(
            exchange_kernel, peers // columns, columns, room, vrows, auxrows, DIRECT
        ),
        in_specs=[pl.BlockSpec(memory_space=pl.ANY)] * 2,
        out_specs=[pl.BlockSpec(memory_space=pl.ANY)] * 4,
        out_shape=[
            jax.ShapeDtypeStruct((peers * room, tile, tile), jnp.bfloat16),
            jax.ShapeDtypeStruct((half * room, tile - DIRECT, tile), jnp.bfloat16),
            jax.ShapeDtypeStruct((peers * auxrows, LANES), jnp.float32),
            jax.ShapeDtypeStruct((half * 8, LANES), jnp.float32),
        ],
        scratch_shapes=[
            pltpu.SemaphoreType.DMA((6, half)),
            pltpu.SemaphoreType.DMA((6, half)),
            pltpu.SemaphoreType.DMA((4,)),
        ],
        compiler_params=pltpu.CompilerParams(
            collective_id=0, has_side_effects=True, vmem_limit_bytes=VMEM_LIMIT
        ),
        name="exchange",
    )(send, aux)

    group = 4 if half % 4 == 0 else 1
    rest = tile - DIRECT
    partial = pl.pallas_call(
        functools.partial(relay_kernel, group, room),
        grid=(half // group,),
        in_specs=[
            pl.BlockSpec((group * 8, LANES), lambda s: (s, 0), memory_space=pltpu.SMEM),
            pl.BlockSpec((group * room, rest, tile), lambda s: (s, 0, 0)),
        ],
        out_specs=pl.BlockSpec((SLOT_DEV, rest, tile), lambda s: (0, 0, 0)),
        scratch_shapes=[pltpu.VMEM((SLOT_DEV, rest, tile), jnp.float32)],
        out_shape=jax.ShapeDtypeStruct((SLOT_DEV, rest, tile), jnp.bfloat16),
        compiler_params=pltpu.CompilerParams(
            dimension_semantics=("arbitrary",), vmem_limit_bytes=VMEM_LIMIT
        ),
        name="relay",
    )(auxrelay, relay)

    part = columns // 2
    other = lax.ppermute(partial, "blk", [(c, (c + part) % columns) for c in range(columns)])

    source = jnp.arange(peers, dtype=jnp.int32) % columns
    close = (source // part == lax.axis_index("blk") // part).astype(jnp.int32)
    summed, loads = pl.pallas_call(
        functools.partial(sum_kernel, group, room, vroom, vrows, DIRECT),
        grid_spec=pltpu.PrefetchScalarGridSpec(
            num_scalar_prefetch=1,
            grid=(peers // group,),
            in_specs=[
                pl.BlockSpec(
                    (group * auxrows, LANES), lambda s, *_: (s, 0), memory_space=pltpu.SMEM
                ),
                pl.BlockSpec((group * room, tile, tile), lambda s, *_: (s, 0, 0)),
                pl.BlockSpec((group * auxrows, LANES), lambda s, *_: (s, 0)),
            ],
            out_specs=[
                pl.BlockSpec((SLOT_DEV, tile, tile), lambda s, *_: (0, 0, 0)),
                pl.BlockSpec((VSLOT_DEV, LANES), whole),
            ],
        ),
        out_shape=[
            jax.ShapeDtypeStruct((SLOT_DEV, tile, tile), jnp.float32),
            jax.ShapeDtypeStruct((VSLOT_DEV, LANES), jnp.float32),
        ],
        compiler_params=pltpu.CompilerParams(
            dimension_semantics=("arbitrary",), vmem_limit_bytes=VMEM_LIMIT
        ),
        cost_estimate=pl.CostEstimate(
            flops=peers * room * tile * tile, bytes_accessed=30_000_000, transcendentals=0
        ),
        name="assemble",
    )(close, auxrecv, recv, auxrecv)

    strip = 16
    assembled = pl.pallas_call(
        add_kernel,
        grid=(rest // strip,),
        in_specs=[
            pl.BlockSpec((SLOT_DEV, strip, tile), lambda s: (0, DIRECT // strip + s, 0)),
            pl.BlockSpec((SLOT_DEV, strip, tile), lambda s: (0, s, 0)),
        ],
        out_specs=pl.BlockSpec((SLOT_DEV, strip, tile), lambda s: (0, DIRECT // strip + s, 0)),
        out_shape=jax.ShapeDtypeStruct((SLOT_DEV, tile, tile), jnp.float32),
        input_output_aliases={0: 0},
        compiler_params=pltpu.CompilerParams(
            dimension_semantics=("arbitrary",), vmem_limit_bytes=VMEM_LIMIT
        ),
        name="add_partial",
    )(summed, other)
    return (assembled, loads)


def solution(mesh):
    in_specs = (
        P(("grp", "blk"), None, None),
        P(("grp", "blk"), None, None),
        P(("grp", "blk"), None, None),
        P(("grp", "blk"), None),
        P(("grp", "blk"), None),
        P(("grp", "blk")),
        P(("grp", "blk"), None, None),
        P(("grp", "blk"), None),
        P(("grp", "blk"), None, None),
        P(("grp", "blk"), None),
    )
    out_specs = (P(("grp", "blk"), None, None), P(("grp", "blk"), None))
    return jax.shard_map(shards, mesh=mesh, in_specs=in_specs, out_specs=out_specs, check_vma=False)
```

```python
import functools

import jax
import jax.numpy as jnp
from jax import lax
from jax.experimental import pallas as pl
from jax.experimental.pallas import tpu as pltpu
from jax.sharding import PartitionSpec as P

BLOCK_UNKNOWNS = 128
SLOT_DEV = 64
VSLOT_DEV = 16
LANES = 128
DIRECT = 64
VMEM_LIMIT = 58 * 1024 * 1024
MESH = pl.DeviceIdType.MESH


def ranks(owner):
    count = owner.shape[0]
    same = owner[:, None] == owner[None, :]
    before = jnp.arange(count)[None, :] < jnp.arange(count)[:, None]
    return jnp.sum((same & before).astype(jnp.int32), axis=1)


def slot_table(owner, rank, slot, live, peers):
    hit = (owner[None, None, :] == jnp.arange(peers, dtype=jnp.int32)[:, None, None]) & (
        rank[None, None, :] == jnp.arange(LANES, dtype=jnp.int32)[None, :, None]
    )
    return jnp.max(jnp.where(hit & live[None, None, :], slot[None, None, :], -1), axis=2)


def condense_kernel(
    emax,
    tiles,
    counts,
    pos,
    vpos,
    factor_ref,
    couple_ref,
    bound_ref,
    inner_ref,
    outer_ref,
    ids_ref,
    send_ref,
    aux_ref,
    held,
    sems,
):
    tile = BLOCK_UNKNOWNS
    e = pl.program_id(0)
    live = counts[0]
    slot = lax.rem(e, 2)

    def drain(which):
        for t in range(tiles * tiles):
            pltpu.make_async_copy(held.at[which, t], send_ref.at[0], sems.at[which, t]).wait()

    @pl.when(e == 0)
    def _():
        aux_ref[...] = ids_ref[...]

    @pl.when(e < live)
    def _():
        factor = factor_ref[0]
        coupled = jnp.dot(factor, couple_ref[0], preferred_element_type=jnp.float32).astype(
            jnp.bfloat16
        )

        def row(ref):
            whole = ref[...].astype(jnp.float32)
            mine = lax.broadcasted_iota(jnp.int32, whole.shape, 0) == e
            return jnp.sum(jnp.where(mine, whole, 0.0), axis=0, keepdims=True)

        inner = jnp.broadcast_to(row(inner_ref), (8, inner_ref.shape[1])).astype(jnp.bfloat16)
        pulled = lax.dot_general(
            inner, factor, (((1,), (1,)), ((), ())), preferred_element_type=jnp.float32
        ).astype(jnp.bfloat16)
        drop = jnp.dot(pulled, coupled, preferred_element_type=jnp.float32)[0:1]
        condensed = (row(outer_ref) - drop).astype(jnp.bfloat16).astype(jnp.float32)
        for a in range(tiles):
            aux_ref[pl.ds(vpos[e * tiles + a], 1), :] = condensed[:, a * tile : (a + 1) * tile]

        product = lax.dot_general(
            coupled, coupled, (((0,), (0,)), ((), ())), preferred_element_type=jnp.float32
        )

        @pl.when(e >= 2)
        def _():
            drain(slot)

        for a in range(tiles):
            rows = slice(a * tile, (a + 1) * tile)
            for b in range(tiles):
                cols = slice(b * tile, (b + 1) * tile)
                t = a * tiles + b
                held[slot, t] = (
                    bound_ref[0, rows, cols].astype(jnp.float32) - product[rows, cols]
                ).astype(jnp.bfloat16)
                pltpu.make_async_copy(
                    held.at[slot, t],
                    send_ref.at[pos[e * tiles * tiles + t]],
                    sems.at[slot, t],
                ).start()

    @pl.when(e == emax - 1)
    def _():
        @pl.when(live >= 2)
        def _():
            drain(lax.rem(live, 2))

        drain(lax.rem(live + 1, 2))


def exchange_kernel(
    groups,
    columns,
    room,
    vrows,
    auxrows,
    direct,
    send,
    aux,
    recv,
    relay,
    auxrecv,
    auxrelay,
    sems,
    auxsems,
    own,
):
    peers = groups * columns
    part = columns // 2
    half = peers // 2
    tile = BLOCK_UNKNOWNS
    g, c = lax.axis_index("grp"), lax.axis_index("blk")
    me = g * columns + c
    base = (c // part) * part
    inner = c % part
    mine = g * part + inner

    def near(j):
        return (g + j // part) % groups, base + (inner + j % part) % part

    def far(j):
        return (g + j // part) % groups, (part - base) + (inner + j % part) % part

    barrier = pltpu.get_barrier_semaphore()

    @pl.loop(1, peers)
    def _(k):
        d = (me + k) % peers
        pl.semaphore_signal(
            barrier, inc=1, device_id=(d // columns, d % columns), device_id_type=MESH
        )

    pl.semaphore_wait(barrier, peers - 1)

    def remote(src, dst, table, kind, j, device):
        return pltpu.make_async_remote_copy(
            src_ref=src,
            dst_ref=dst,
            send_sem=table.at[2 * kind, j],
            recv_sem=table.at[2 * kind + 1, j],
            device_id=device,
            device_id_type=MESH,
        )

    def flat(device):
        return device[0] * columns + device[1]

    def near_copies(j):
        device = near(j)
        d = flat(device)
        return (
            remote(
                send.at[pl.ds(d * room, room)],
                recv.at[pl.ds(me * room, room)],
                sems, 0, j, device,
            ),
            remote(
                aux.at[pl.ds(d * auxrows, auxrows)],
                auxrecv.at[pl.ds(me * auxrows, auxrows)],
                auxsems, 0, j, device,
            ),
        )

    def far_copies(j):
        device = far(j)
        d = flat(device)
        return (
            remote(
                send.at[pl.ds(d * room, room), pl.ds(0, direct)],
                recv.at[pl.ds(me * room, room), pl.ds(0, direct)],
                sems, 1, j, device,
            ),
            remote(
                aux.at[pl.ds(d * auxrows, auxrows)],
                auxrecv.at[pl.ds(me * auxrows, auxrows)],
                auxsems, 1, j, device,
            ),
        )

    def relay_copies(j):
        device = near(j)
        d = flat(far(j))
        return (
            remote(
                send.at[pl.ds(d * room, room), pl.ds(direct, tile - direct)],
                relay.at[pl.ds(mine * room, room)],
                sems, 2, j, device,
            ),
            remote(
                aux.at[pl.ds(d * auxrows + vrows, 8)],
                auxrelay.at[pl.ds(mine * 8, 8)],
                auxsems, 2, j, device,
            ),
        )

    @pl.loop(0, half)
    def _(j):
        for copy in far_copies(j):
            copy.start()
        r = (j + half // 3) % half
        n = (j + 2 * half // 3) % half

        @pl.when(r > 0)
        def _():
            for copy in relay_copies(r):
                copy.start()

        @pl.when(n > 0)
        def _():
            for copy in near_copies(n):
                copy.start()

    twin = flat(far(0))
    local = (
        pltpu.make_async_copy(
            send.at[pl.ds(me * room, room)], recv.at[pl.ds(me * room, room)], own.at[0]
        ),
        pltpu.make_async_copy(
            aux.at[pl.ds(me * auxrows, auxrows)],
            auxrecv.at[pl.ds(me * auxrows, auxrows)],
            own.at[1],
        ),
        pltpu.make_async_copy(
            send.at[pl.ds(twin * room, room), pl.ds(direct, tile - direct)],
            relay.at[pl.ds(mine * room, room)],
            own.at[2],
        ),
        pltpu.make_async_copy(
            aux.at[pl.ds(twin * auxrows + vrows, 8)], auxrelay.at[pl.ds(mine * 8, 8)], own.at[3]
        ),
    )
    for copy in local:
        copy.start()
    for copy in local:
        copy.wait()
    for copy in far_copies(0):
        copy.wait()

    @pl.loop(1, half)
    def _(j):
        for copy in far_copies(j) + relay_copies(j) + near_copies(j):
            copy.wait()


def relay_kernel(group, room, ids, relay_ref, out_ref, total):
    step = pl.program_id(0)

    @pl.when(step == 0)
    def _():
        total[...] = jnp.zeros_like(total)

    for p in range(group):

        @pl.loop(0, room)
        def _(r):
            target = ids[p * 8, r].astype(jnp.int32)

            @pl.when(target >= 0)
            def _():
                total[target] += relay_ref[p * room + r].astype(jnp.float32)

    @pl.when(step == pl.num_programs(0) - 1)
    def _():
        out_ref[...] = total[...].astype(out_ref.dtype)


def sum_kernel(
    group, room, vroom, vrows, direct, close, ids, recv_ref, aux_ref, out_ref, loads_ref
):
    step = pl.program_id(0)
    auxrows = vrows + 8

    @pl.when(step == 0)
    def _():
        out_ref[...] = jnp.zeros_like(out_ref)
        loads_ref[...] = jnp.zeros_like(loads_ref)

    for p in range(group):
        first = p * auxrows
        whole = close[step * group + p] > 0

        for v in range(vroom):
            slot = ids[first + vrows + 1, v].astype(jnp.int32)

            @pl.when(slot >= 0)
            def _():
                loads_ref[pl.ds(slot, 1), :] += aux_ref[pl.ds(first + v, 1), :]

        @pl.when(whole)
        def _():
            @pl.loop(0, room)
            def _(r):
                target = ids[first + vrows, r].astype(jnp.int32)

                @pl.when(target >= 0)
                def _():
                    out_ref[target] += recv_ref[p * room + r].astype(jnp.float32)

        @pl.when(jnp.logical_not(whole))
        def _():
            @pl.loop(0, room)
            def _(r):
                target = ids[first + vrows, r].astype(jnp.int32)

                @pl.when(target >= 0)
                def _():
                    out_ref[target, :direct, :] += recv_ref[p * room + r, :direct, :].astype(
                        jnp.float32
                    )


def add_kernel(sum_ref, far_ref, out_ref):
    out_ref[...] = sum_ref[...] + far_ref[...].astype(jnp.float32)


def shards(
    inv_factor,
    coupling,
    boundary,
    load_int,
    load_bnd,
    counts,
    tile_owner,
    tile_slot,
    vec_owner,
    vec_slot,
):
    emax, ni, _ = inv_factor.shape
    nb = boundary.shape[1]
    tile = BLOCK_UNKNOWNS
    tiles = nb // tile
    columns = lax.axis_size("blk")
    peers = lax.axis_size("grp") * columns
    ntiles = emax * tiles * tiles
    room = max(2, 3 * ntiles // (2 * peers))
    vroom = max(2, 3 * emax * tiles // (2 * peers))
    vrows = -(-vroom // 8) * 8
    auxrows = vrows + 8

    owner = tile_owner.reshape(-1)
    vowner = vec_owner.reshape(-1)
    rank, vrank = ranks(owner), ranks(vowner)
    pos = owner * room + rank
    vpos = vowner * auxrows + vrank
    live = jnp.arange(ntiles) < counts[0] * (tiles * tiles)
    vlive = jnp.arange(emax * tiles) < counts[0] * tiles
    ids = slot_table(owner, rank, tile_slot.reshape(-1), live, peers)
    vids = slot_table(vowner, vrank, vec_slot.reshape(-1), vlive, peers)
    at = lax.broadcasted_iota(jnp.int32, (1, auxrows, 1), 1)
    table = jnp.where(
        at == vrows, ids[:, None, :], jnp.where(at == vrows + 1, vids[:, None, :], 0)
    )
    table = table.astype(jnp.float32).reshape(peers * auxrows, LANES)

    def element(e, cnt, *_):
        return (jnp.minimum(e, cnt[0] - 1), 0, 0)

    def whole(*_):
        return (0, 0)

    send, aux = pl.pallas_call(
        functools.partial(condense_kernel, emax, tiles),
        grid_spec=pltpu.PrefetchScalarGridSpec(
            num_scalar_prefetch=3,
            grid=(emax,),
            in_specs=[
                pl.BlockSpec((1, ni, ni), element),
                pl.BlockSpec((1, ni, nb), element),
                pl.BlockSpec((1, nb, nb), element),
                pl.BlockSpec((emax, ni), whole),
                pl.BlockSpec((emax, nb), whole),
                pl.BlockSpec((peers * auxrows, LANES), whole),
            ],
            out_specs=[
                pl.BlockSpec(memory_space=pl.ANY),
                pl.BlockSpec((peers * auxrows, LANES), whole),
            ],
            scratch_shapes=[
                pltpu.VMEM((2, tiles * tiles, tile, tile), jnp.bfloat16),
                pltpu.SemaphoreType.DMA((2, tiles * tiles)),
            ],
        ),
        out_shape=[
            jax.ShapeDtypeStruct((peers * room, tile, tile), jnp.bfloat16),
            jax.ShapeDtypeStruct((peers * auxrows, LANES), jnp.float32),
        ],
        compiler_params=pltpu.CompilerParams(
            dimension_semantics=("arbitrary",), vmem_limit_bytes=VMEM_LIMIT
        ),
        name="condense",
    )(counts, pos, vpos, inv_factor, coupling, boundary, load_int, load_bnd, table)

    half = peers // 2
    recv, relay, auxrecv, auxrelay = pl.pallas_call(
        functools.partial(
            exchange_kernel, peers // columns, columns, room, vrows, auxrows, DIRECT
        ),
        in_specs=[pl.BlockSpec(memory_space=pl.ANY)] * 2,
        out_specs=[pl.BlockSpec(memory_space=pl.ANY)] * 4,
        out_shape=[
            jax.ShapeDtypeStruct((peers * room, tile, tile), jnp.bfloat16),
            jax.ShapeDtypeStruct((half * room, tile - DIRECT, tile), jnp.bfloat16),
            jax.ShapeDtypeStruct((peers * auxrows, LANES), jnp.float32),
            jax.ShapeDtypeStruct((half * 8, LANES), jnp.float32),
        ],
        scratch_shapes=[
            pltpu.SemaphoreType.DMA((6, half)),
            pltpu.SemaphoreType.DMA((6, half)),
            pltpu.SemaphoreType.DMA((4,)),
        ],
        compiler_params=pltpu.CompilerParams(
            collective_id=0, has_side_effects=True, vmem_limit_bytes=VMEM_LIMIT
        ),
        name="exchange",
    )(send, aux)

    group = 4 if half % 4 == 0 else 1
    rest = tile - DIRECT
    partial = pl.pallas_call(
        functools.partial(relay_kernel, group, room),
        grid=(half // group,),
        in_specs=[
            pl.BlockSpec((group * 8, LANES), lambda s: (s, 0), memory_space=pltpu.SMEM),
            pl.BlockSpec((group * room, rest, tile), lambda s: (s, 0, 0)),
        ],
        out_specs=pl.BlockSpec((SLOT_DEV, rest, tile), lambda s: (0, 0, 0)),
        scratch_shapes=[pltpu.VMEM((SLOT_DEV, rest, tile), jnp.float32)],
        out_shape=jax.ShapeDtypeStruct((SLOT_DEV, rest, tile), jnp.bfloat16),
        compiler_params=pltpu.CompilerParams(
            dimension_semantics=("arbitrary",), vmem_limit_bytes=VMEM_LIMIT
        ),
        name="relay",
    )(auxrelay, relay)

    part = columns // 2
    other = lax.ppermute(partial, "blk", [(c, (c + part) % columns) for c in range(columns)])

    source = jnp.arange(peers, dtype=jnp.int32) % columns
    close = (source // part == lax.axis_index("blk") // part).astype(jnp.int32)
    summed, loads = pl.pallas_call(
        functools.partial(sum_kernel, group, room, vroom, vrows, DIRECT),
        grid_spec=pltpu.PrefetchScalarGridSpec(
            num_scalar_prefetch=1,
            grid=(peers // group,),
            in_specs=[
                pl.BlockSpec(
                    (group * auxrows, LANES), lambda s, *_: (s, 0), memory_space=pltpu.SMEM
                ),
                pl.BlockSpec((group * room, tile, tile), lambda s, *_: (s, 0, 0)),
                pl.BlockSpec((group * auxrows, LANES), lambda s, *_: (s, 0)),
            ],
            out_specs=[
                pl.BlockSpec((SLOT_DEV, tile, tile), lambda s, *_: (0, 0, 0)),
                pl.BlockSpec((VSLOT_DEV, LANES), whole),
            ],
        ),
        out_shape=[
            jax.ShapeDtypeStruct((SLOT_DEV, tile, tile), jnp.float32),
            jax.ShapeDtypeStruct((VSLOT_DEV, LANES), jnp.float32),
        ],
        compiler_params=pltpu.CompilerParams(
            dimension_semantics=("arbitrary",), vmem_limit_bytes=VMEM_LIMIT
        ),
        cost_estimate=pl.CostEstimate(
            flops=peers * room * tile * tile, bytes_accessed=30_000_000, transcendentals=0
        ),
        name="assemble",
    )(close, auxrecv, recv, auxrecv)

    strip = 16
    assembled = pl.pallas_call(
        add_kernel,
        grid=(rest // strip,),
        in_specs=[
            pl.BlockSpec((SLOT_DEV, strip, tile), lambda s: (0, DIRECT // strip + s, 0)),
            pl.BlockSpec((SLOT_DEV, strip, tile), lambda s: (0, s, 0)),
        ],
        out_specs=pl.BlockSpec((SLOT_DEV, strip, tile), lambda s: (0, DIRECT // strip + s, 0)),
        out_shape=jax.ShapeDtypeStruct((SLOT_DEV, tile, tile), jnp.float32),
        input_output_aliases={0: 0},
        compiler_params=pltpu.CompilerParams(
            dimension_semantics=("arbitrary",), vmem_limit_bytes=VMEM_LIMIT
        ),
        name="add_partial",
    )(summed, other)
    return (assembled, loads)


def solution(mesh):
    in_specs = (
        P(("grp", "blk"), None, None),
        P(("grp", "blk"), None, None),
        P(("grp", "blk"), None, None),
        P(("grp", "blk"), None),
        P(("grp", "blk"), None),
        P(("grp", "blk")),
        P(("grp", "blk"), None, None),
        P(("grp", "blk"), None),
        P(("grp", "blk"), None, None),
        P(("grp", "blk"), None),
    )
    out_specs = (P(("grp", "blk"), None, None), P(("grp", "blk"), None))
    return jax.shard_map(shards, mesh=mesh, in_specs=in_specs, out_specs=out_specs, check_vma=False)
```

```python
import functools

import jax
import jax.numpy as jnp
from jax import lax
from jax.experimental import pallas as pl
from jax.experimental.pallas import tpu as pltpu
from jax.sharding import PartitionSpec as P

BLOCK_UNKNOWNS = 128
SLOT_DEV = 64
VSLOT_DEV = 16
LANES = 128
DIRECT = 32
VMEM_LIMIT = 58 * 1024 * 1024
MESH = pl.DeviceIdType.MESH


def ranks(owner):
    count = owner.shape[0]
    same = owner[:, None] == owner[None, :]
    before = jnp.arange(count)[None, :] < jnp.arange(count)[:, None]
    return jnp.sum((same & before).astype(jnp.int32), axis=1)


def slot_table(owner, rank, slot, live, peers):
    hit = (owner[None, None, :] == jnp.arange(peers, dtype=jnp.int32)[:, None, None]) & (
        rank[None, None, :] == jnp.arange(LANES, dtype=jnp.int32)[None, :, None]
    )
    return jnp.max(jnp.where(hit & live[None, None, :], slot[None, None, :], -1), axis=2)


def condense_kernel(
    emax,
    tiles,
    counts,
    pos,
    vpos,
    factor_ref,
    couple_ref,
    bound_ref,
    inner_ref,
    outer_ref,
    ids_ref,
    send_ref,
    aux_ref,
    held,
    sems,
):
    tile = BLOCK_UNKNOWNS
    e = pl.program_id(0)
    live = counts[0]
    slot = lax.rem(e, 2)

    def drain(which):
        for t in range(tiles * tiles):
            pltpu.make_async_copy(held.at[which, t], send_ref.at[0], sems.at[which, t]).wait()

    @pl.when(e == 0)
    def _():
        aux_ref[...] = ids_ref[...]

    @pl.when(e < live)
    def _():
        factor = factor_ref[0]
        coupled = jnp.dot(factor, couple_ref[0], preferred_element_type=jnp.float32).astype(
            jnp.bfloat16
        )

        def row(ref):
            whole = ref[...].astype(jnp.float32)
            mine = lax.broadcasted_iota(jnp.int32, whole.shape, 0) == e
            return jnp.sum(jnp.where(mine, whole, 0.0), axis=0, keepdims=True)

        inner = jnp.broadcast_to(row(inner_ref), (8, inner_ref.shape[1])).astype(jnp.bfloat16)
        pulled = lax.dot_general(
            inner, factor, (((1,), (1,)), ((), ())), preferred_element_type=jnp.float32
        ).astype(jnp.bfloat16)
        drop = jnp.dot(pulled, coupled, preferred_element_type=jnp.float32)[0:1]
        condensed = (row(outer_ref) - drop).astype(jnp.bfloat16).astype(jnp.float32)
        for a in range(tiles):
            aux_ref[pl.ds(vpos[e * tiles + a], 1), :] = condensed[:, a * tile : (a + 1) * tile]

        product = lax.dot_general(
            coupled, coupled, (((0,), (0,)), ((), ())), preferred_element_type=jnp.float32
        )

        @pl.when(e >= 2)
        def _():
            drain(slot)

        for a in range(tiles):
            rows = slice(a * tile, (a + 1) * tile)
            for b in range(tiles):
                cols = slice(b * tile, (b + 1) * tile)
                t = a * tiles + b
                held[slot, t] = (
                    bound_ref[0, rows, cols].astype(jnp.float32) - product[rows, cols]
                ).astype(jnp.bfloat16)
                pltpu.make_async_copy(
                    held.at[slot, t],
                    send_ref.at[pos[e * tiles * tiles + t]],
                    sems.at[slot, t],
                ).start()

    @pl.when(e == emax - 1)
    def _():
        @pl.when(live >= 2)
        def _():
            drain(lax.rem(live, 2))

        drain(lax.rem(live + 1, 2))


def exchange_kernel(
    groups,
    columns,
    room,
    vrows,
    auxrows,
    direct,
    send,
    aux,
    recv,
    relay,
    auxnear,
    auxfar,
    auxrelay,
    sems,
    auxsems,
    own,
):
    peers = groups * columns
    part = columns // 2
    half = peers // 2
    tile = BLOCK_UNKNOWNS
    g, c = lax.axis_index("grp"), lax.axis_index("blk")
    me = g * columns + c
    base = (c // part) * part
    inner = c % part
    mine = g * part + inner

    def near(j):
        return (g + j // part) % groups, base + (inner + j % part) % part

    def far(j):
        return (g + j // part) % groups, (part - base) + (inner + j % part) % part

    barrier = pltpu.get_barrier_semaphore()

    @pl.loop(1, peers)
    def _(k):
        d = (me + k) % peers
        pl.semaphore_signal(
            barrier, inc=1, device_id=(d // columns, d % columns), device_id_type=MESH
        )

    pl.semaphore_wait(barrier, peers - 1)

    def remote(src, dst, table, kind, j, device):
        return pltpu.make_async_remote_copy(
            src_ref=src,
            dst_ref=dst,
            send_sem=table.at[2 * kind, j],
            recv_sem=table.at[2 * kind + 1, j],
            device_id=device,
            device_id_type=MESH,
        )

    def flat(device):
        return device[0] * columns + device[1]

    def near_copies(j):
        device = near(j)
        return (
            remote(
                aux.at[pl.ds(flat(device) * auxrows, auxrows)],
                auxnear.at[pl.ds(mine * auxrows, auxrows)],
                auxsems, 0, j, device,
            ),
        )

    def far_copies(j):
        device = far(j)
        d = flat(device)
        return (
            remote(
                send.at[pl.ds(d * room, room), pl.ds(0, direct)],
                recv.at[pl.ds(mine * room, room)],
                sems, 1, j, device,
            ),
            remote(
                aux.at[pl.ds(d * auxrows, auxrows)],
                auxfar.at[pl.ds(mine * auxrows, auxrows)],
                auxsems, 1, j, device,
            ),
        )

    def relay_copies(j):
        device = near(j)
        d = flat(far(j))
        return (
            remote(
                send.at[pl.ds(d * room, room), pl.ds(direct, tile - direct)],
                relay.at[pl.ds(mine * room, room)],
                sems, 2, j, device,
            ),
            remote(
                aux.at[pl.ds(d * auxrows + vrows, 8)],
                auxrelay.at[pl.ds(mine * 8, 8)],
                auxsems, 2, j, device,
            ),
        )

    @pl.loop(0, half)
    def _(j):
        for copy in far_copies(j):
            copy.start()
        r = (j + half // 3) % half
        n = (j + 2 * half // 3) % half

        @pl.when(r > 0)
        def _():
            for copy in relay_copies(r):
                copy.start()

        @pl.when(n > 0)
        def _():
            for copy in near_copies(n):
                copy.start()

    twin = flat(far(0))
    local = (
        pltpu.make_async_copy(
            aux.at[pl.ds(me * auxrows, auxrows)],
            auxnear.at[pl.ds(mine * auxrows, auxrows)],
            own.at[0],
        ),
        pltpu.make_async_copy(
            send.at[pl.ds(twin * room, room), pl.ds(direct, tile - direct)],
            relay.at[pl.ds(mine * room, room)],
            own.at[1],
        ),
        pltpu.make_async_copy(
            aux.at[pl.ds(twin * auxrows + vrows, 8)], auxrelay.at[pl.ds(mine * 8, 8)], own.at[2]
        ),
    )
    for copy in local:
        copy.start()
    for copy in local:
        copy.wait()
    for copy in far_copies(0):
        copy.wait()

    @pl.loop(1, half)
    def _(j):
        for copy in far_copies(j) + relay_copies(j) + near_copies(j):
            copy.wait()


def swap_kernel(groups, columns, room, send, partial, recv, other, sems, own):
    part = columns // 2
    half = groups * part
    g, c = lax.axis_index("grp"), lax.axis_index("blk")
    base = (c // part) * part
    inner = c % part
    me, mine = g * columns + c, g * part + inner

    def near(j):
        return (g + j // part) % groups, base + (inner + j % part) % part

    twin = (g, (c + part) % columns)
    barrier = pltpu.get_barrier_semaphore()
    pl.semaphore_signal(barrier, inc=1, device_id=twin, device_id_type=MESH)

    @pl.loop(1, half)
    def _(j):
        pl.semaphore_signal(barrier, inc=1, device_id=near(j), device_id_type=MESH)

    pl.semaphore_wait(barrier, half)

    def near_copy(j):
        device = near(j)
        d = device[0] * columns + device[1]
        return pltpu.make_async_remote_copy(
            src_ref=send.at[pl.ds(d * room, room)],
            dst_ref=recv.at[pl.ds(mine * room, room)],
            send_sem=sems.at[0, j],
            recv_sem=sems.at[1, j],
            device_id=device,
            device_id_type=MESH,
        )

    swap = pltpu.make_async_remote_copy(
        src_ref=partial,
        dst_ref=other,
        send_sem=sems.at[0, 0],
        recv_sem=sems.at[1, 0],
        device_id=twin,
        device_id_type=MESH,
    )
    swap.start()

    @pl.loop(1, half)
    def _(j):
        near_copy(j).start()

    local = pltpu.make_async_copy(
        send.at[pl.ds(me * room, room)], recv.at[pl.ds(mine * room, room)], own.at[0]
    )
    local.start()
    local.wait()
    swap.wait()

    @pl.loop(1, half)
    def _(j):
        near_copy(j).wait()


def relay_kernel(group, room, ids, relay_ref, out_ref, total):
    step = pl.program_id(0)

    @pl.when(step == 0)
    def _():
        total[...] = jnp.zeros_like(total)

    for p in range(group):

        @pl.loop(0, room)
        def _(r):
            target = ids[p * 8, r].astype(jnp.int32)

            @pl.when(target >= 0)
            def _():
                total[target] += relay_ref[p * room + r].astype(jnp.float32)

    @pl.when(step == pl.num_programs(0) - 1)
    def _():
        out_ref[...] = total[...].astype(out_ref.dtype)


def sum_kernel(
    group,
    room,
    vroom,
    vrows,
    direct,
    near_ids,
    far_ids,
    near_ref,
    far_ref,
    near_aux,
    far_aux,
    other_ref,
    out_ref,
    loads_ref,
):
    auxrows = vrows + 8

    @pl.when(pl.program_id(0) == 0)
    def _():
        out_ref[:, :direct, :] = jnp.zeros((SLOT_DEV, direct, LANES), jnp.float32)
        out_ref[:, direct:, :] = other_ref[...].astype(jnp.float32)
        loads_ref[...] = jnp.zeros_like(loads_ref)

    for p in range(group):
        first = p * auxrows

        for ids, aux_ref in ((near_ids, near_aux), (far_ids, far_aux)):
            for v in range(vroom):
                slot = ids[first + vrows + 1, v].astype(jnp.int32)

                @pl.when(slot >= 0)
                def _():
                    loads_ref[pl.ds(slot, 1), :] += aux_ref[pl.ds(first + v, 1), :]

        @pl.loop(0, room)
        def _(r):
            target = near_ids[first + vrows, r].astype(jnp.int32)
            beyond = far_ids[first + vrows, r].astype(jnp.int32)

            @pl.when(target >= 0)
            def _():
                out_ref[target] += near_ref[p * room + r].astype(jnp.float32)

            @pl.when(beyond >= 0)
            def _():
                out_ref[beyond, :direct, :] += far_ref[p * room + r].astype(jnp.float32)


def shards(
    inv_factor,
    coupling,
    boundary,
    load_int,
    load_bnd,
    counts,
    tile_owner,
    tile_slot,
    vec_owner,
    vec_slot,
):
    emax, ni, _ = inv_factor.shape
    nb = boundary.shape[1]
    tile = BLOCK_UNKNOWNS
    tiles = nb // tile
    columns = lax.axis_size("blk")
    peers = lax.axis_size("grp") * columns
    ntiles = emax * tiles * tiles
    room = max(2, 3 * ntiles // (2 * peers))
    vroom = max(2, 3 * emax * tiles // (2 * peers))
    vrows = -(-vroom // 8) * 8
    auxrows = vrows + 8

    owner = tile_owner.reshape(-1)
    vowner = vec_owner.reshape(-1)
    rank, vrank = ranks(owner), ranks(vowner)
    pos = owner * room + rank
    vpos = vowner * auxrows + vrank
    live = jnp.arange(ntiles) < counts[0] * (tiles * tiles)
    vlive = jnp.arange(emax * tiles) < counts[0] * tiles
    ids = slot_table(owner, rank, tile_slot.reshape(-1), live, peers)
    vids = slot_table(vowner, vrank, vec_slot.reshape(-1), vlive, peers)
    at = lax.broadcasted_iota(jnp.int32, (1, auxrows, 1), 1)
    table = jnp.where(
        at == vrows, ids[:, None, :], jnp.where(at == vrows + 1, vids[:, None, :], 0)
    )
    table = table.astype(jnp.float32).reshape(peers * auxrows, LANES)

    def element(e, cnt, *_):
        return (jnp.minimum(e, cnt[0] - 1), 0, 0)

    def whole(*_):
        return (0, 0)

    send, aux = pl.pallas_call(
        functools.partial(condense_kernel, emax, tiles),
        grid_spec=pltpu.PrefetchScalarGridSpec(
            num_scalar_prefetch=3,
            grid=(emax,),
            in_specs=[
                pl.BlockSpec((1, ni, ni), element),
                pl.BlockSpec((1, ni, nb), element),
                pl.BlockSpec((1, nb, nb), element),
                pl.BlockSpec((emax, ni), whole),
                pl.BlockSpec((emax, nb), whole),
                pl.BlockSpec((peers * auxrows, LANES), whole),
            ],
            out_specs=[
                pl.BlockSpec(memory_space=pl.ANY),
                pl.BlockSpec((peers * auxrows, LANES), whole),
            ],
            scratch_shapes=[
                pltpu.VMEM((2, tiles * tiles, tile, tile), jnp.bfloat16),
                pltpu.SemaphoreType.DMA((2, tiles * tiles)),
            ],
        ),
        out_shape=[
            jax.ShapeDtypeStruct((peers * room, tile, tile), jnp.bfloat16),
            jax.ShapeDtypeStruct((peers * auxrows, LANES), jnp.float32),
        ],
        compiler_params=pltpu.CompilerParams(
            dimension_semantics=("arbitrary",), vmem_limit_bytes=VMEM_LIMIT
        ),
        name="condense",
    )(counts, pos, vpos, inv_factor, coupling, boundary, load_int, load_bnd, table)

    half = peers // 2
    far, relay, auxnear, auxfar, auxrelay = pl.pallas_call(
        functools.partial(
            exchange_kernel, peers // columns, columns, room, vrows, auxrows, DIRECT
        ),
        in_specs=[pl.BlockSpec(memory_space=pl.ANY)] * 2,
        out_specs=[pl.BlockSpec(memory_space=pl.ANY)] * 5,
        out_shape=[
            jax.ShapeDtypeStruct((half * room, DIRECT, tile), jnp.bfloat16),
            jax.ShapeDtypeStruct((half * room, tile - DIRECT, tile), jnp.bfloat16),
            jax.ShapeDtypeStruct((half * auxrows, LANES), jnp.float32),
            jax.ShapeDtypeStruct((half * auxrows, LANES), jnp.float32),
            jax.ShapeDtypeStruct((half * 8, LANES), jnp.float32),
        ],
        scratch_shapes=[
            pltpu.SemaphoreType.DMA((6, half)),
            pltpu.SemaphoreType.DMA((6, half)),
            pltpu.SemaphoreType.DMA((3,)),
        ],
        compiler_params=pltpu.CompilerParams(
            collective_id=0, has_side_effects=True, vmem_limit_bytes=VMEM_LIMIT
        ),
        name="exchange",
    )(send, aux)

    group = 4 if half % 4 == 0 else 1
    rest = tile - DIRECT
    partial = pl.pallas_call(
        functools.partial(relay_kernel, group, room),
        grid=(half // group,),
        in_specs=[
            pl.BlockSpec((group * 8, LANES), lambda s: (s, 0), memory_space=pltpu.SMEM),
            pl.BlockSpec((group * room, rest, tile), lambda s: (s, 0, 0)),
        ],
        out_specs=pl.BlockSpec((SLOT_DEV, rest, tile), lambda s: (0, 0, 0)),
        scratch_shapes=[pltpu.VMEM((SLOT_DEV, rest, tile), jnp.float32)],
        out_shape=jax.ShapeDtypeStruct((SLOT_DEV, rest, tile), jnp.bfloat16),
        compiler_params=pltpu.CompilerParams(
            dimension_semantics=("arbitrary",), vmem_limit_bytes=VMEM_LIMIT
        ),
        name="relay",
    )(auxrelay, relay)

    recv, other = pl.pallas_call(
        functools.partial(swap_kernel, peers // columns, columns, room),
        in_specs=[pl.BlockSpec(memory_space=pl.ANY)] * 2,
        out_specs=[pl.BlockSpec(memory_space=pl.ANY)] * 2,
        out_shape=[
            jax.ShapeDtypeStruct((half * room, tile, tile), jnp.bfloat16),
            jax.ShapeDtypeStruct(partial.shape, jnp.bfloat16),
        ],
        scratch_shapes=[
            pltpu.SemaphoreType.DMA((2, half)),
            pltpu.SemaphoreType.DMA((1,)),
        ],
        compiler_params=pltpu.CompilerParams(
            collective_id=1, has_side_effects=True, vmem_limit_bytes=VMEM_LIMIT
        ),
        name="swap",
    )(send, partial)

    def ids_block():
        return pl.BlockSpec((group * auxrows, LANES), lambda s: (s, 0), memory_space=pltpu.SMEM)

    def aux_block():
        return pl.BlockSpec((group * auxrows, LANES), lambda s: (s, 0))

    assembled, loads = pl.pallas_call(
        functools.partial(sum_kernel, group, room, vroom, vrows, DIRECT),
        grid=(half // group,),
        in_specs=[
            ids_block(),
            ids_block(),
            pl.BlockSpec((group * room, tile, tile), lambda s: (s, 0, 0)),
            pl.BlockSpec((group * room, DIRECT, tile), lambda s: (s, 0, 0)),
            aux_block(),
            aux_block(),
            pl.BlockSpec((SLOT_DEV, rest, tile), lambda s: (0, 0, 0)),
        ],
        out_specs=[
            pl.BlockSpec((SLOT_DEV, tile, tile), lambda s: (0, 0, 0)),
            pl.BlockSpec((VSLOT_DEV, LANES), whole),
        ],
        out_shape=[
            jax.ShapeDtypeStruct((SLOT_DEV, tile, tile), jnp.float32),
            jax.ShapeDtypeStruct((VSLOT_DEV, LANES), jnp.float32),
        ],
        compiler_params=pltpu.CompilerParams(
            dimension_semantics=("arbitrary",), vmem_limit_bytes=VMEM_LIMIT
        ),
        name="assemble",
    )(auxnear, auxfar, recv, far, auxnear, auxfar, other)
    return (assembled, loads)


def solution(mesh):
    in_specs = (
        P(("grp", "blk"), None, None),
        P(("grp", "blk"), None, None),
        P(("grp", "blk"), None, None),
        P(("grp", "blk"), None),
        P(("grp", "blk"), None),
        P(("grp", "blk")),
        P(("grp", "blk"), None, None),
        P(("grp", "blk"), None),
        P(("grp", "blk"), None, None),
        P(("grp", "blk"), None),
    )
    out_specs = (P(("grp", "blk"), None, None), P(("grp", "blk"), None))
    return jax.shard_map(shards, mesh=mesh, in_specs=in_specs, out_specs=out_specs, check_vma=False)
```
